32 devices in a mesh: groups: 2 (over y), dp: 4 (over z), tensor: 4 (over x, core).
Axes of the slice: x: 2, y: 2, z: 4, core: 2. Of those that a mesh axis runs over, the one named last changes fastest.
Arguments:
- acts: bfloat16 [2048, 8192], P(('groups', 'dp'), 'tensor'), parts along dimension 0, may hold values from -6 to 6
- output_gradient: bfloat16 [2048, 4096], P(('groups', 'dp'), 'tensor'), parts along dimension 0, may hold values from -6 to 6
- frozen_weight: bfloat16 [8192, 4096], P('tensor', 'dp'), may hold values from -0.09375 to 0.09375
- adapter_down_weights: bfloat16 [64, 16, 8192], P('dp', None, 'tensor'), may hold values from -0.25 to 0.25
- adapter_up_weights: bfloat16 [64, 16, 4096], P('dp', None, 'tensor'), may hold values from -0.09375 to 0.09375
- block_adapter_index: int32 [16], P('groups'), parts along dimension 0, may hold values from 0 to 63, as said below
- adapter_slot_index: int32 [64], replicated, may hold values from 0 to 63, each once
Outputs:
- in_grad: bfloat16 [2048, 8192], P(('groups', 'dp'), 'tensor'), parts along dimension 0
- owned_down: float32 [128, 16, 8192], P(('groups', 'dp'), None, 'tensor'), parts along dimension 0
- owned_up: float32 [128, 16, 4096], P(('groups', 'dp'), None, 'tensor'), parts along dimension 0
The draws below stay inside these ranges and needn't reach their ends.
There are 2 independent parts, one for each index of `groups`. The reference program is written for one: setup_inputs(seed, part) draws one part's arguments, and reference() takes and returns one part's arrays. A program takes and returns all parts, laid end to end along the dimension named above; an argument that names none is the same for every part. Nothing has to cross between parts.
Inputs may be any that keep to these rules, and one draw needn't show every extreme that they name: `block_adapter_index`: never falls from one block to the next; blocks of one adapter stand together. `adapter_slot_index`: each slot is named once.
All inputs are finite; a program needn't handle non-finite values.
Results may differ from the reference program's by a relative error of at most 0.005.
Values may be sent and summed in bfloat16 or wider, within the bound.
A program may use at most 128 MiB of HBM per device.

```python
import jax
import jax.numpy as jnp

INPUT_WIDTH = 8192
OUTPUT_WIDTH = 4096
ADAPTER_RANK = 16
ADAPTER_COUNT = 64
BLOCK_TOKENS = 128
TOKENS = 1024


def draw_block_adapter_index(key, part):
    key = jax.random.fold_in(key, 11)
    first_key, second_key = jax.random.split(key)
    left_ids = jax.random.randint(first_key, (TOKENS // BLOCK_TOKENS,), 0, ADAPTER_COUNT)
    right_ids = jax.random.randint(second_key, (TOKENS // BLOCK_TOKENS,), 0, ADAPTER_COUNT)
    picked = jnp.minimum(left_ids, right_ids)
    picked = picked.at[0].set(0).at[-1].set(ADAPTER_COUNT - 1)
    return jnp.sort(picked).astype(jnp.int32)


def block_scale(key, extent, shards, smallest, largest):
    level, own = 1.0, jax.random.fold_in(key, 6)
    for axis_at, blocks in shards:
        draws = jnp.exp(jax.random.uniform(jax.random.fold_in(own, axis_at), (blocks,), jnp.float32, smallest / len(shards), largest / len(shards)))
        level = level * jnp.repeat(draws, extent[axis_at] // blocks).reshape([-1 if axis == axis_at else 1 for axis in range(len(extent))])
    return level


def noise(rng, shape, width, most, pieces=(), dtype=jnp.bfloat16):
    result = jax.random.normal(rng, shape, jnp.float32) * width
    if len(pieces) > 0:
        result = block_scale(rng, shape, pieces, -0.22, 0.18) * result
    return jnp.clip(result, min=-most, max=most).astype(dtype)


def setup_inputs(seed: int = 0, part: int = 0) -> dict:
    key_of = jax.random.split(jax.random.key(seed), 8)
    part_keys = jax.random.split(jax.random.fold_in(key_of[7], part), 8)
    acts = noise(part_keys[0], (TOKENS, INPUT_WIDTH), 1.0, 6.0, ((0, 4), (1, 4)))
    output_gradient = noise(part_keys[1], (TOKENS, OUTPUT_WIDTH), 1.0, 6.0, ((0, 4), (1, 4)))
    frozen_weight = noise(key_of[2], (INPUT_WIDTH, OUTPUT_WIDTH), OUTPUT_WIDTH ** -0.5, 0.09375, ((0, 4), (1, 4)))
    adapter_down_weights = noise(key_of[3], (ADAPTER_COUNT, ADAPTER_RANK, INPUT_WIDTH), (INPUT_WIDTH // 16) ** -0.5, 0.25, ((0, 4), (2, 4)))
    adapter_up_weights = noise(key_of[4], (ADAPTER_COUNT, ADAPTER_RANK, OUTPUT_WIDTH), OUTPUT_WIDTH ** -0.5, 0.09375, ((0, 4), (2, 4)))
    block_adapter_index = draw_block_adapter_index(jax.random.fold_in(jax.random.fold_in(key_of[7], part), 71), part)
    adapter_slot_index = jax.random.permutation(key_of[6], ADAPTER_COUNT).astype(jnp.int32)
    return {"acts": acts, "output_gradient": output_gradient, "frozen_weight": frozen_weight, "adapter_down_weights": adapter_down_weights, "adapter_up_weights": adapter_up_weights, "block_adapter_index": block_adapter_index, "adapter_slot_index": adapter_slot_index}


ADAPTER_SCALE = 2.0


def reference(acts, output_gradient, frozen_weight, adapter_down_weights, adapter_up_weights, block_adapter_index, adapter_slot_index):
    num_blocks = block_adapter_index.shape[0]
    active_block_rows = acts.astype(jnp.float32).reshape(num_blocks, BLOCK_TOKENS, INPUT_WIDTH)
    grad_blocks = output_gradient.astype(jnp.float32).reshape(num_blocks, BLOCK_TOKENS, OUTPUT_WIDTH)
    adapter_down_factor = adapter_down_weights[adapter_slot_index]
    adapter_up_factor = adapter_up_weights[adapter_slot_index]
    selected_down = adapter_down_factor[block_adapter_index].astype(jnp.float32)
    up_sel = adapter_up_factor[block_adapter_index].astype(jnp.float32)
    reduced_rank_output = jnp.einsum("ctx,cyx->cty", active_block_rows, selected_down)
    back_rank = jnp.einsum("bko,bro->bkr", grad_blocks, up_sel)
    lowrank_b = reduced_rank_output.astype(jnp.bfloat16)
    backward_block = back_rank.astype(jnp.bfloat16)
    widened_gradient = ADAPTER_SCALE * jnp.einsum("aex,axq->aeq", backward_block.astype(jnp.float32), selected_down)
    widened_gradient = widened_gradient.reshape(num_blocks * BLOCK_TOKENS, INPUT_WIDTH)
    in_grad = (jnp.dot(output_gradient, frozen_weight.T, preferred_element_type=jnp.float32) + widened_gradient).astype(jnp.bfloat16)
    factor_matrix = ADAPTER_SCALE / BLOCK_TOKENS
    block_down_factor = (factor_matrix * jnp.einsum("aqw,aqg->awg", backward_block.astype(jnp.float32), active_block_rows)).astype(jnp.bfloat16)
    block_up = (factor_matrix * jnp.einsum("bkr,bko->bro", lowrank_b.astype(jnp.float32), grad_blocks)).astype(jnp.bfloat16)
    grad_down = jax.ops.segment_sum(block_down_factor.astype(jnp.float32), block_adapter_index, num_segments=ADAPTER_COUNT)
    grad_up = jax.ops.segment_sum(block_up.astype(jnp.float32), block_adapter_index, num_segments=ADAPTER_COUNT)
    owned_down = jnp.zeros_like(grad_down).at[adapter_slot_index].set(grad_down)
    owned_up = jnp.zeros_like(grad_up).at[adapter_slot_index].set(grad_up)
    return in_grad, owned_down, owned_up
```

```python
import functools

import jax
import jax.numpy as jnp
from jax import lax
from jax.experimental import pallas as pl
from jax.experimental.pallas import tpu as pltpu
from jax.sharding import PartitionSpec as P

BLOCK_TOKENS = 128


ADAPTER_SCALE = 2.0


MESH = pl.DeviceIdType.MESH
NT = (((1,), (1,)), ((), ()))
NN = (((1,), (0,)), ((), ()))
RANK = 16


def chain_order(dp):
    table = []
    for own in range(dp):
        up, down = list(range(dp - 1, own, -1)), list(range(own))
        first, second = (up, down) if len(up) >= len(down) else (down, up)
        merged = []
        while first or second:
            if first:
                merged.append(first.pop(0))
            if second:
                merged.append(second.pop(0))
        table.append(merged)
    return table


def fused_kernel(
    dp, tensor, chunks,
    block_ref, slot_ref, acts_ref, og_ref, w_ref, down_ref, up_ref,
    grad_ref, own_down_ref, own_up_ref,
    og_all, partial, arrived, total, sel_send, sel_recv, rank_mine, rank_recv, pieces,
    og_send, og_near, og_far, og_relay, og_recv,
    sel_ssem, sel_rsem, rank_ssem, rank_rsem, piece_ssem, piece_rsem, part_ssem, part_rsem,
):
    d, t = lax.axis_index("dp"), lax.axis_index("tensor")
    rows, in_cols = acts_ref.shape
    out_cols = og_ref.shape[1]
    nblk = rows // BLOCK_TOKENS
    nslot = down_ref.shape[0]
    quarter = rows // tensor
    width = in_cols // chunks
    sib, across = t + 1 - 2 * (t % 2), (t + 2) % tensor
    across_sib = across + 1 - 2 * (across % 2)

    table = chain_order(dp)
    order = []
    for k in range(dp - 1):
        at = jnp.int32(table[0][k])
        for i in range(1, dp):
            at = jnp.where(d == i, table[i][k], at)
        order.append(at)

    def wait(ref, sem):
        pltpu.make_async_copy(ref, ref, sem).wait()

    def send(src, dst, ssem, rsem, to):
        copy = pltpu.make_async_remote_copy(
            src_ref=src, dst_ref=dst, send_sem=ssem, recv_sem=rsem, device_id=to, device_id_type=MESH
        )
        copy.start()
        return copy

    barrier = pltpu.get_barrier_semaphore()
    for i in range(1, dp * tensor):
        peer = (d * tensor + t + i) % (dp * tensor)
        pl.semaphore_signal(
            barrier, inc=1, device_id={"dp": peer // tensor, "tensor": peer % tensor}, device_id_type=MESH
        )
    pl.semaphore_wait(barrier, dp * tensor - 1)

    def og_rows(q):
        return pl.ds(pl.multiple_of(q * quarter, quarter), quarter)

    stays = [jnp.logical_and(t == d, t == q) for q in range(tensor)]
    for q in range(tensor):
        src, dst = og_ref.at[og_rows(q)], og_all.at[d, og_rows(q)]

        @pl.when(stays[q])
        def _():
            pltpu.make_async_copy(src, dst, og_recv.at[d, q]).start()

        @pl.when(jnp.logical_not(stays[q]))
        def _():
            send(src, dst, og_send.at[q], og_recv.at[d, q], {"dp": t, "tensor": q})

    slots = [slot_ref[block_ref[b]] for b in range(dp * nblk)]
    for b in range(dp * nblk):
        here = slots[b] - d * nslot
        own = jnp.logical_and(here >= 0, here < nslot)
        at = jnp.clip(here, 0, nslot - 1)
        dn, up = down_ref[at], up_ref[at]
        r = pl.ds((b % nblk) * RANK, RANK)
        sel_send[b // nblk, r, :in_cols] = jnp.where(own, dn, jnp.zeros_like(dn))
        sel_send[b // nblk, r, in_cols:] = jnp.where(own, up, jnp.zeros_like(up))
    waits = []
    for j in range(1, dp):
        peer = (d + j) % dp
        waits.append(send(sel_send.at[peer], sel_recv.at[d], sel_ssem.at[j - 1], sel_rsem.at[d], {"dp": peer}))

    fetch_order = order + [d]
    for k, row in enumerate(fetch_order):
        piece = og_all.at[row, og_rows(t)]
        wait(piece, og_recv.at[row, t])
        waits.append(send(piece, piece, og_far.at[k], og_recv.at[row, t], {"tensor": across}))
        waits.append(send(piece, piece, og_near.at[k], og_recv.at[row, t], {"tensor": sib}))

    sel = sel_send[d]
    for j in range(1, dp):
        peer = (d + j) % dp
        wait(sel_recv.at[peer], sel_rsem.at[peer])
        sel = sel + sel_recv[peer]
    sel_recv[d] = sel
    for c in range(nblk):
        r, tok = pl.ds(c * RANK, RANK), pl.ds(c * BLOCK_TOKENS, BLOCK_TOKENS)
        low = lax.dot_general(sel_recv[d, r, :in_cols], acts_ref[tok, :], NT, preferred_element_type=jnp.float32)
        back = lax.dot_general(sel_recv[d, r, in_cols:], og_ref[tok, :], NT, preferred_element_type=jnp.float32)
        rank_mine[pl.ds(c * RANK, RANK), :] = low
        rank_mine[pl.ds((nblk + c) * RANK, RANK), :] = back
    for j in range(1, tensor):
        peer = (t + j) % tensor
        waits.append(send(rank_mine, rank_recv.at[t], rank_ssem.at[j - 1], rank_rsem.at[t], {"tensor": peer}))

    for k, row in enumerate(fetch_order):
        piece = og_all.at[row, og_rows(across)]
        wait(piece, og_recv.at[row, across])
        waits.append(send(piece, piece, og_relay.at[k], og_recv.at[row, across], {"tensor": sib}))

    rank = rank_mine[...]
    for j in range(1, tensor):
        peer = (t + j) % tensor
        wait(rank_recv.at[peer], rank_rsem.at[peer])
        rank = rank + rank_recv[peer]
    rank_b = rank.astype(jnp.bfloat16)
    factor = ADAPTER_SCALE / BLOCK_TOKENS
    back_t = []
    for c in range(nblk):
        tok = pl.ds(c * BLOCK_TOKENS, BLOCK_TOKENS)
        low_b = rank_b[c * RANK:(c + 1) * RANK, :]
        back_b = rank_b[(nblk + c) * RANK:(nblk + c + 1) * RANK, :]
        at = pl.ds(pl.multiple_of((d * nblk + c) * RANK, RANK), RANK)
        pieces[at, :in_cols] = (
            factor * lax.dot_general(back_b, acts_ref[tok, :], NN, preferred_element_type=jnp.float32)
        ).astype(jnp.bfloat16)
        pieces[at, in_cols:] = (
            factor * lax.dot_general(low_b, og_ref[tok, :], NN, preferred_element_type=jnp.float32)
        ).astype(jnp.bfloat16)
        back_t.append(rank[(nblk + c) * RANK:(nblk + c + 1) * RANK, :].T.astype(jnp.bfloat16))
    mine = pl.ds(pl.multiple_of(d * nblk * RANK, nblk * RANK), nblk * RANK)
    for j in range(1, dp):
        peer = (d + j) % dp
        waits.append(send(pieces.at[mine], pieces.at[mine], piece_ssem.at[j - 1], piece_rsem.at[d], {"dp": peer}))

    def product(row, c):
        tile = w_ref[pl.ds(pl.multiple_of(c * width, width), width), :]
        return lax.dot_general(og_all[row], tile, NT, preferred_element_type=jnp.float32)

    for k, row in enumerate(order):
        for q in (sib, across_sib):
            wait(og_all.at[row, og_rows(q)], og_recv.at[row, q])
        upward = row > d
        fed = jnp.logical_or(jnp.logical_and(upward, d > 0), jnp.logical_and(row < d, d < dp - 1))
        to = jnp.where(upward, d + 1, d - 1)
        lands = jnp.where(row == d - 1, dp, row)

        @pl.loop(0, chunks)
        def _(c):
            total[...] = product(row, c)

            @pl.when(fed)
            def _():
                wait(arrived.at[row, c], part_rsem.at[row, c])
                total[...] += arrived[row, c].astype(jnp.float32)

            partial[k, c] = total[...].astype(jnp.bfloat16)
            send(partial.at[k, c], arrived.at[lands, c], part_ssem.at[k, c], part_rsem.at[lands, c], {"dp": to})

    for j in range(1, dp):
        peer = (d + j) % dp
        theirs = pl.ds(pl.multiple_of(peer * nblk * RANK, nblk * RANK), nblk * RANK)
        wait(pieces.at[theirs], piece_rsem.at[peer])
    shape = (nslot * RANK, dp * nblk * RANK)
    line, column = lax.broadcasted_iota(jnp.int32, shape, 0), lax.broadcasted_iota(jnp.int32, shape, 1)
    goal = jnp.full(shape, -1, jnp.int32)
    for b in range(dp * nblk):
        goal = jnp.where(column // RANK == b, (slots[b] - d * nslot) * RANK + column % RANK, goal)
    chooser = jnp.where(goal == line, 1.0, 0.0).astype(jnp.bfloat16)
    own_down_ref[...] = lax.dot_general(chooser, pieces[:, :in_cols], NN, preferred_element_type=jnp.float32)
    own_up_ref[...] = lax.dot_general(chooser, pieces[:, in_cols:], NN, preferred_element_type=jnp.float32)

    for q in (sib, across_sib):
        wait(og_all.at[d, og_rows(q)], og_recv.at[d, q])
    for c in range(chunks):
        cols = pl.ds(c * width, width)
        total[...] = product(d, c)
        for i in range(nblk):
            tok = pl.ds(i * BLOCK_TOKENS, BLOCK_TOKENS)
            total[tok, :] += ADAPTER_SCALE * lax.dot_general(
                back_t[i], sel_recv[d, pl.ds(i * RANK, RANK), cols], NN, preferred_element_type=jnp.float32
            )

        @pl.when(d > 0)
        def _():
            wait(arrived.at[d, c], part_rsem.at[d, c])
            total[...] += arrived[d, c].astype(jnp.float32)

        @pl.when(d < dp - 1)
        def _():
            wait(arrived.at[dp, c], part_rsem.at[dp, c])
            total[...] += arrived[dp, c].astype(jnp.float32)

        grad_ref[:, cols] = total[...].astype(jnp.bfloat16)

    for copy in waits:
        copy.wait_send()
    for q in range(tensor):
        @pl.when(jnp.logical_not(stays[q]))
        def _():
            wait(og_ref.at[og_rows(q)], og_send.at[q])
    for k in range(dp - 1):
        for c in range(chunks):
            wait(partial.at[k, c], part_ssem.at[k, c])


def fused(dp, tensor, acts, og, w, down, up, blocks, slots):
    rows, in_cols = acts.shape
    out_cols = og.shape[1]
    nslot, nblk, chunks = down.shape[0], rows // BLOCK_TOKENS, 4
    width = in_cols // chunks
    vmem, smem = pl.BlockSpec(memory_space=pltpu.VMEM), pl.BlockSpec(memory_space=pltpu.SMEM)
    dma = pltpu.SemaphoreType.DMA
    grad, own_down, own_up = pl.pallas_call(
        functools.partial(fused_kernel, dp, tensor, chunks),
        out_shape=(
            jax.ShapeDtypeStruct((rows, in_cols), jnp.bfloat16),
            jax.ShapeDtypeStruct((nslot * RANK, in_cols), jnp.float32),
            jax.ShapeDtypeStruct((nslot * RANK, out_cols), jnp.float32),
        ),
        in_specs=[smem, smem] + [vmem] * 5,
        out_specs=(vmem, vmem, vmem),
        scratch_shapes=[
            pltpu.VMEM((dp, rows, w.shape[1]), jnp.bfloat16),
            pltpu.VMEM((dp - 1, chunks, rows, width), jnp.bfloat16),
            pltpu.VMEM((dp + 1, chunks, rows, width), jnp.bfloat16),
            pltpu.VMEM((rows, width), jnp.float32),
            pltpu.VMEM((dp, nblk * RANK, in_cols + out_cols), jnp.bfloat16),
            pltpu.VMEM((dp, nblk * RANK, in_cols + out_cols), jnp.bfloat16),
            pltpu.VMEM((2 * nblk * RANK, BLOCK_TOKENS), jnp.float32),
            pltpu.VMEM((tensor, 2 * nblk * RANK, BLOCK_TOKENS), jnp.float32),
            pltpu.VMEM((dp * nblk * RANK, in_cols + out_cols), jnp.bfloat16),
            dma((tensor,)), dma((dp,)), dma((dp,)), dma((dp,)), dma((dp, tensor)),
            dma((dp - 1,)), dma((dp,)), dma((tensor - 1,)), dma((tensor,)),
            dma((dp - 1,)), dma((dp,)), dma((dp - 1, chunks)), dma((dp + 1, chunks)),
        ],
        compiler_params=pltpu.CompilerParams(
            collective_id=0, has_side_effects=True, vmem_limit_bytes=48 * 1024 * 1024
        ),
        cost_estimate=pl.CostEstimate(
            flops=2 * dp * rows * in_cols * w.shape[1], bytes_accessed=12 * 1024 * 1024, transcendentals=0
        ),
    )(blocks, slots, acts, og, w, down, up)
    return grad, own_down.reshape(nslot, RANK, in_cols), own_up.reshape(nslot, RANK, out_cols)


def per_device(
    acts,
    output_gradient,
    frozen_weight,
    adapter_down_weights,
    adapter_up_weights,
    block_adapter_index,
    adapter_slot_index,
):
    tok_rows, in_cols = acts.shape
    out_cols = output_gradient.shape[1]
    blocks_dev = tok_rows // BLOCK_TOKENS
    own_index = lax.axis_index("dp")
    per_holder_sums = adapter_down_weights.shape[0]
    my_blocks = lax.dynamic_slice_in_dim(block_adapter_index, own_index * blocks_dev, blocks_dev)
    all_down, all_up = (
        lax.all_gather(adapter_down_weights, "dp", axis=0, tiled=True),
        lax.all_gather(adapter_up_weights, "dp", axis=0, tiled=True),
    )
    my_slots = adapter_slot_index[my_blocks]
    selected_down = all_down[my_slots]
    up_sel = all_up[my_slots]
    active_block_rows = acts.reshape(blocks_dev, BLOCK_TOKENS, in_cols)
    grad_blocks = output_gradient.reshape(blocks_dev, BLOCK_TOKENS, out_cols)
    down_portion = jnp.einsum(
        "ctx,cyx->cty", active_block_rows, selected_down, preferred_element_type=jnp.float32
    )
    up_part = jnp.einsum("bko,bro->bkr", grad_blocks, up_sel, preferred_element_type=jnp.float32)
    reduced_rank_output, back_rank = lax.psum((down_portion, up_part), "tensor")
    lowrank_b = reduced_rank_output.astype(jnp.bfloat16)
    backward_block = back_rank.astype(jnp.bfloat16)
    widened_gradient = ADAPTER_SCALE * jnp.einsum(
        "aex,axq->aeq", backward_block, selected_down, preferred_element_type=jnp.float32
    )
    widened_gradient = widened_gradient.reshape(tok_rows, in_cols)
    full_grad = lax.all_gather(output_gradient, "tensor", axis=1, tiled=True)
    in_grad = (
        widened_gradient
        + lax.dot_general(
            full_grad,
            lax.all_gather(frozen_weight, "dp", axis=1, tiled=True),
            (((1,), (1,)), ((), ())),
            preferred_element_type=jnp.float32,
        )
    ).astype(jnp.bfloat16)
    factor_matrix = ADAPTER_SCALE / BLOCK_TOKENS
    grad_down = (
        factor_matrix
        * jnp.einsum(
            "aqw,aqg->awg", backward_block, active_block_rows, preferred_element_type=jnp.float32
        )
    ).astype(jnp.bfloat16)
    grad_up = (
        factor_matrix
        * jnp.einsum("bkr,bko->bro", lowrank_b, grad_blocks, preferred_element_type=jnp.float32)
    ).astype(jnp.bfloat16)
    slot_range = jnp.arange(per_holder_sums, dtype=jnp.int32)
    base_slot = own_index * per_holder_sums
    piece_down = lax.all_gather(grad_down, "dp", axis=0, tiled=True)
    piece_up = lax.all_gather(grad_up, "dp", axis=0, tiled=True)
    slot_local = adapter_slot_index[block_adapter_index] - base_slot
    chooser = (slot_local[:, None] == slot_range[None, :]).astype(jnp.bfloat16)
    new_down = jnp.einsum("ns,nrd->srd", chooser, piece_down, preferred_element_type=jnp.float32)
    new_up = jnp.einsum("ns,nro->sro", chooser, piece_up, preferred_element_type=jnp.float32)
    return (in_grad, new_down, new_up)


def solution(mesh):
    dp, tensor = mesh.shape["dp"], mesh.shape["tensor"]

    def step(acts, og, w, down, up, blocks, slots):
        if dp == tensor == 4:
            return fused(dp, tensor, acts, og, w, down, up, blocks, slots)
        return per_device(acts, og, w, down, up, blocks, slots)

    return jax.shard_map(
        step,
        mesh=mesh,
        in_specs=(
            P(("groups", "dp"), "tensor"),
            P(("groups", "dp"), "tensor"),
            P("tensor", "dp"),
            P("dp", None, "tensor"),
            P("dp", None, "tensor"),
            P("groups"),
            P(),
        ),
        out_specs=(
            P(("groups", "dp"), "tensor"),
            P(("groups", "dp"), None, "tensor"),
            P(("groups", "dp"), None, "tensor"),
        ),
        check_vma=False,
    )
```

```python
import functools

import jax
import jax.numpy as jnp
from jax import lax
from jax.experimental import pallas as pl
from jax.experimental.pallas import tpu as pltpu
from jax.sharding import PartitionSpec as P

BLOCK_TOKENS = 128


ADAPTER_SCALE = 2.0


MESH = pl.DeviceIdType.MESH
NT = (((1,), (1,)), ((), ()))
NN = (((1,), (0,)), ((), ()))
RANK = 16


def chain_order(dp):
    table = []
    for own in range(dp):
        up, down = list(range(dp - 1, own, -1)), list(range(own))
        first, second = (up, down) if len(up) >= len(down) else (down, up)
        merged = []
        while first or second:
            if first:
                merged.append(first.pop(0))
            if second:
                merged.append(second.pop(0))
        table.append(merged)
    return table


def fused_kernel(
    dp, tensor, chunks,
    block_ref, slot_ref, acts_hbm, og_hbm, w_hbm, down_hbm, up_hbm,
    grad_ref, own_down_ref, own_up_ref,
    acts_ref, og_ref, w_ref, down_ref, up_ref,
    og_all, partial, arrived, total, own_total, sel_send, sel_recv, rank_mine, rank_recv, pieces,
    load_sem, og_send, og_near, og_far, og_relay, og_recv,
    sel_ssem, sel_rsem, rank_ssem, rank_rsem, piece_ssem, piece_rsem, part_ssem, part_rsem,
):
    d, t = lax.axis_index("dp"), lax.axis_index("tensor")
    rows, in_cols = acts_ref.shape
    nblk = rows // BLOCK_TOKENS
    nslot = down_ref.shape[0]
    quarter, half = rows // tensor, rows // 2
    width = in_cols // chunks
    sib, across = t + 1 - 2 * (t % 2), (t + 2) % tensor
    across_sib = across + 1 - 2 * (across % 2)
    x = t // 2

    table = chain_order(dp)
    order = []
    for k in range(dp - 1):
        at = jnp.int32(table[0][k])
        for i in range(1, dp):
            at = jnp.where(d == i, table[i][k], at)
        order.append(at)

    def wait(ref, sem):
        pltpu.make_async_copy(ref, ref, sem).wait()

    def send(src, dst, ssem, rsem, to):
        copy = pltpu.make_async_remote_copy(
            src_ref=src, dst_ref=dst, send_sem=ssem, recv_sem=rsem, device_id=to, device_id_type=MESH
        )
        copy.start()
        return copy

    loads = [
        pltpu.make_async_copy(src, dst, load_sem.at[i])
        for i, (src, dst) in enumerate(
            ((down_hbm, down_ref), (up_hbm, up_ref), (w_hbm, w_ref), (acts_hbm, acts_ref), (og_hbm, og_ref))
        )
    ]
    for load in loads:
        load.start()

    barrier = pltpu.get_barrier_semaphore()
    for i in range(1, dp * tensor):
        peer = (d * tensor + t + i) % (dp * tensor)
        pl.semaphore_signal(
            barrier, inc=1, device_id={"dp": peer // tensor, "tensor": peer % tensor}, device_id_type=MESH
        )
    pl.semaphore_wait(barrier, dp * tensor - 1)

    def og_rows(q):
        return pl.ds(pl.multiple_of(q * quarter, quarter), quarter)

    stays = [jnp.logical_and(t == d, t == q) for q in range(tensor)]
    for q in range(tensor):
        src, dst = og_hbm.at[og_rows(q)], og_all.at[d, og_rows(q)]

        @pl.when(stays[q])
        def _():
            pltpu.make_async_copy(src, dst, og_recv.at[d, q]).start()

        @pl.when(jnp.logical_not(stays[q]))
        def _():
            send(src, dst, og_send.at[q], og_recv.at[d, q], {"dp": t, "tensor": q})

    slots = [slot_ref[block_ref[b]] for b in range(dp * nblk)]
    loads[0].wait()
    loads[1].wait()
    for b in range(dp * nblk):
        here = slots[b] - d * nslot
        own = jnp.logical_and(here >= 0, here < nslot)
        at = jnp.clip(here, 0, nslot - 1)
        dn, up = down_ref[at], up_ref[at]
        r = pl.ds((b % nblk) * RANK, RANK)
        sel_send[b // nblk, r, :in_cols] = jnp.where(own, dn, jnp.zeros_like(dn))
        sel_send[b // nblk, r, in_cols:] = jnp.where(own, up, jnp.zeros_like(up))
    waits = []

    fetch_order = order + [d]
    for k, row in enumerate(fetch_order):
        piece = og_all.at[row, og_rows(t)]
        wait(piece, og_recv.at[row, t])
        waits.append(send(piece, piece, og_near.at[k], og_recv.at[row, t], {"tensor": sib}))
        waits.append(send(piece, piece, og_far.at[k], og_recv.at[row, t], {"tensor": across}))

    for j in range(1, dp):
        peer = (d + j) % dp
        waits.append(send(sel_send.at[peer], sel_recv.at[d], sel_ssem.at[j - 1], sel_rsem.at[d], {"dp": peer}))

    def half_rows(h):
        place = x if h == 0 else 1 - x
        return pl.ds(pl.multiple_of(place * half, half), half)

    def relay_sums(k, h):
        row = order[k]
        wait(og_all.at[row, og_rows(sib if h == 0 else across_sib)], og_recv.at[row, sib if h == 0 else across_sib])
        upward = row > d
        fed = jnp.logical_or(jnp.logical_and(upward, d > 0), jnp.logical_and(row < d, d < dp - 1))
        to = jnp.where(upward, d + 1, d - 1)
        lands = jnp.where(row == d - 1, dp, row)

        @pl.loop(0, chunks)
        def _(c):
            i = h * chunks + c
            tile = w_ref[pl.ds(pl.multiple_of(c * width, width), width), :]
            total[...] = lax.dot_general(
                og_all[row, half_rows(h), :], tile, NT, preferred_element_type=jnp.float32
            )

            @pl.when(fed)
            def _():
                wait(arrived.at[row, i], part_rsem.at[row, i])
                total[...] += arrived[row, i].astype(jnp.float32)

            partial[k, i] = total[...].astype(jnp.bfloat16)
            send(partial.at[k, i], arrived.at[lands, i], part_ssem.at[k, i], part_rsem.at[lands, i], {"dp": to})

    loads[2].wait()
    relay_sums(0, 0)

    for k, row in enumerate(fetch_order):
        piece = og_all.at[row, og_rows(across)]
        wait(piece, og_recv.at[row, across])
        waits.append(send(piece, piece, og_relay.at[k], og_recv.at[row, across], {"tensor": sib}))

    relay_sums(1, 0)

    loads[3].wait()
    loads[4].wait()
    sel = sel_send[d]
    for j in range(1, dp):
        peer = (d + j) % dp
        wait(sel_recv.at[peer], sel_rsem.at[peer])
        sel = sel + sel_recv[peer]
    sel_recv[d] = sel
    for c in range(nblk):
        r, tok = pl.ds(c * RANK, RANK), pl.ds(c * BLOCK_TOKENS, BLOCK_TOKENS)
        low = lax.dot_general(sel_recv[d, r, :in_cols], acts_ref[tok, :], NT, preferred_element_type=jnp.float32)
        back = lax.dot_general(sel_recv[d, r, in_cols:], og_ref[tok, :], NT, preferred_element_type=jnp.float32)
        rank_mine[pl.ds(c * RANK, RANK), :] = low
        rank_mine[pl.ds((nblk + c) * RANK, RANK), :] = back
    for j in range(1, tensor):
        peer = (t + j) % tensor
        waits.append(send(rank_mine, rank_recv.at[t], rank_ssem.at[j - 1], rank_rsem.at[t], {"tensor": peer}))

    relay_sums(2, 0)

    rank = rank_mine[...]
    for j in range(1, tensor):
        peer = (t + j) % tensor
        wait(rank_recv.at[peer], rank_rsem.at[peer])
        rank = rank + rank_recv[peer]
    rank_b = rank.astype(jnp.bfloat16)
    factor = ADAPTER_SCALE / BLOCK_TOKENS
    back_t = []
    for c in range(nblk):
        tok = pl.ds(c * BLOCK_TOKENS, BLOCK_TOKENS)
        low_b = rank_b[c * RANK:(c + 1) * RANK, :]
        back_b = rank_b[(nblk + c) * RANK:(nblk + c + 1) * RANK, :]
        pieces[d, pl.ds(c * RANK, RANK), :in_cols] = (
            factor * lax.dot_general(back_b, acts_ref[tok, :], NN, preferred_element_type=jnp.float32)
        ).astype(jnp.bfloat16)
        pieces[d, pl.ds(c * RANK, RANK), in_cols:] = (
            factor * lax.dot_general(low_b, og_ref[tok, :], NN, preferred_element_type=jnp.float32)
        ).astype(jnp.bfloat16)
        back_t.append(rank[(nblk + c) * RANK:(nblk + c + 1) * RANK, :].T.astype(jnp.bfloat16))

    def pass_on(j, take, give):
        for way, (has, more, step) in enumerate(((d >= j, d < dp - 1, 1), (d + j < dp, d > 0, -1))):
            at = jnp.clip(d - step * j, 0, dp - 1)

            if take:
                @pl.when(has)
                def _():
                    wait(pieces.at[at], piece_rsem.at[at])

            if give is not None:
                @pl.when(jnp.logical_and(has, more))
                def _():
                    if give:
                        send(
                            pieces.at[at], pieces.at[at], piece_ssem.at[way, j], piece_rsem.at[at],
                            {"dp": jnp.clip(d + step, 0, dp - 1)},
                        )
                    else:
                        wait(pieces.at[at], piece_ssem.at[way, j])

    pass_on(0, False, True)
    for k in range(dp - 1):
        relay_sums(k, 1)
        pass_on(k + 1, True, True if k + 1 < dp - 1 else None)

    for q in (sib, across_sib):
        wait(og_all.at[d, og_rows(q)], og_recv.at[d, q])
    for c in range(chunks):
        cols = pl.ds(c * width, width)
        own_total[:, cols] = lax.dot_general(
            og_all[d], w_ref[cols, :], NT, preferred_element_type=jnp.float32
        )
        for i in range(nblk):
            tok = pl.ds(i * BLOCK_TOKENS, BLOCK_TOKENS)
            own_total[tok, cols] += ADAPTER_SCALE * lax.dot_general(
                back_t[i], sel_recv[d, pl.ds(i * RANK, RANK), cols], NN, preferred_element_type=jnp.float32
            )

    shape = (nslot * RANK, nblk * RANK)
    line, column = lax.broadcasted_iota(jnp.int32, shape, 0), lax.broadcasted_iota(jnp.int32, shape, 1)
    choosers = []
    for r in range(dp):
        goal = jnp.full(shape, -1, jnp.int32)
        for b in range(nblk):
            goal = jnp.where(
                column // RANK == b, (slots[r * nblk + b] - d * nslot) * RANK + column % RANK, goal
            )
        choosers.append(jnp.where(goal == line, 1.0, 0.0).astype(jnp.bfloat16))
    chooser = jnp.concatenate(choosers, axis=1)
    all_pieces = pieces[...].reshape(dp * nblk * RANK, pieces.shape[2])
    own_down_ref[...] = lax.dot_general(chooser, all_pieces[:, :in_cols], NN, preferred_element_type=jnp.float32)
    own_up_ref[...] = lax.dot_general(chooser, all_pieces[:, in_cols:], NN, preferred_element_type=jnp.float32)

    for h in range(2):
        for c in range(chunks):
            i, cols = h * chunks + c, pl.ds(c * width, width)
            spot = half_rows(h)

            @pl.when(d > 0)
            def _():
                wait(arrived.at[d, i], part_rsem.at[d, i])
                own_total[spot, cols] += arrived[d, i].astype(jnp.float32)

            @pl.when(d < dp - 1)
            def _():
                wait(arrived.at[dp, i], part_rsem.at[dp, i])
                own_total[spot, cols] += arrived[dp, i].astype(jnp.float32)

            grad_ref[spot, cols] = own_total[spot, cols].astype(jnp.bfloat16)

    for copy in waits:
        copy.wait_send()
    for j in range(dp - 1):
        pass_on(j, False, False)
    for q in range(tensor):
        @pl.when(jnp.logical_not(stays[q]))
        def _():
            wait(og_ref.at[og_rows(q)], og_send.at[q])
    for k in range(dp - 1):
        for c in range(2 * chunks):
            wait(partial.at[k, c], part_ssem.at[k, c])


def fused(dp, tensor, acts, og, w, down, up, blocks, slots):
    rows, in_cols = acts.shape
    out_cols = og.shape[1]
    nslot, nblk, chunks = down.shape[0], rows // BLOCK_TOKENS, 4
    width, half = in_cols // chunks, rows // 2
    vmem, smem = pl.BlockSpec(memory_space=pltpu.VMEM), pl.BlockSpec(memory_space=pltpu.SMEM)
    hbm = pl.BlockSpec(memory_space=pltpu.HBM)
    dma = pltpu.SemaphoreType.DMA
    grad, own_down, own_up = pl.pallas_call(
        functools.partial(fused_kernel, dp, tensor, chunks),
        out_shape=(
            jax.ShapeDtypeStruct((rows, in_cols), jnp.bfloat16),
            jax.ShapeDtypeStruct((nslot * RANK, in_cols), jnp.float32),
            jax.ShapeDtypeStruct((nslot * RANK, out_cols), jnp.float32),
        ),
        in_specs=[smem, smem] + [hbm] * 5,
        out_specs=(vmem, vmem, vmem),
        scratch_shapes=[
            pltpu.VMEM(acts.shape, jnp.bfloat16),
            pltpu.VMEM(og.shape, jnp.bfloat16),
            pltpu.VMEM(w.shape, jnp.bfloat16),
            pltpu.VMEM(down.shape, jnp.bfloat16),
            pltpu.VMEM(up.shape, jnp.bfloat16),
            pltpu.VMEM((dp, rows, w.shape[1]), jnp.bfloat16),
            pltpu.VMEM((dp - 1, 2 * chunks, half, width), jnp.bfloat16),
            pltpu.VMEM((dp + 1, 2 * chunks, half, width), jnp.bfloat16),
            pltpu.VMEM((half, width), jnp.float32),
            pltpu.VMEM((rows, in_cols), jnp.float32),
            pltpu.VMEM((dp, nblk * RANK, in_cols + out_cols), jnp.bfloat16),
            pltpu.VMEM((dp, nblk * RANK, in_cols + out_cols), jnp.bfloat16),
            pltpu.VMEM((2 * nblk * RANK, BLOCK_TOKENS), jnp.float32),
            pltpu.VMEM((tensor, 2 * nblk * RANK, BLOCK_TOKENS), jnp.float32),
            pltpu.VMEM((dp, nblk * RANK, in_cols + out_cols), jnp.bfloat16),
            dma((5,)), dma((tensor,)), dma((dp,)), dma((dp,)), dma((dp,)), dma((dp, tensor)),
            dma((dp - 1,)), dma((dp,)), dma((tensor - 1,)), dma((tensor,)),
            dma((2, dp - 1)), dma((dp,)), dma((dp - 1, 2 * chunks)), dma((dp + 1, 2 * chunks)),
        ],
        compiler_params=pltpu.CompilerParams(
            collective_id=0, has_side_effects=True, vmem_limit_bytes=48 * 1024 * 1024
        ),
        cost_estimate=pl.CostEstimate(
            flops=2 * dp * rows * in_cols * w.shape[1], bytes_accessed=12 * 1024 * 1024, transcendentals=0
        ),
    )(blocks, slots, acts, og, w, down, up)
    return grad, own_down.reshape(nslot, RANK, in_cols), own_up.reshape(nslot, RANK, out_cols)


def per_device(
    acts,
    output_gradient,
    frozen_weight,
    adapter_down_weights,
    adapter_up_weights,
    block_adapter_index,
    adapter_slot_index,
):
    tok_rows, in_cols = acts.shape
    out_cols = output_gradient.shape[1]
    blocks_dev = tok_rows // BLOCK_TOKENS
    own_index = lax.axis_index("dp")
    per_holder_sums = adapter_down_weights.shape[0]
    my_blocks = lax.dynamic_slice_in_dim(block_adapter_index, own_index * blocks_dev, blocks_dev)
    all_down, all_up = (
        lax.all_gather(adapter_down_weights, "dp", axis=0, tiled=True),
        lax.all_gather(adapter_up_weights, "dp", axis=0, tiled=True),
    )
    my_slots = adapter_slot_index[my_blocks]
    selected_down = all_down[my_slots]
    up_sel = all_up[my_slots]
    active_block_rows = acts.reshape(blocks_dev, BLOCK_TOKENS, in_cols)
    grad_blocks = output_gradient.reshape(blocks_dev, BLOCK_TOKENS, out_cols)
    down_portion = jnp.einsum(
        "ctx,cyx->cty", active_block_rows, selected_down, preferred_element_type=jnp.float32
    )
    up_part = jnp.einsum("bko,bro->bkr", grad_blocks, up_sel, preferred_element_type=jnp.float32)
    reduced_rank_output, back_rank = lax.psum((down_portion, up_part), "tensor")
    lowrank_b = reduced_rank_output.astype(jnp.bfloat16)
    backward_block = back_rank.astype(jnp.bfloat16)
    widened_gradient = ADAPTER_SCALE * jnp.einsum(
        "aex,axq->aeq", backward_block, selected_down, preferred_element_type=jnp.float32
    )
    widened_gradient = widened_gradient.reshape(tok_rows, in_cols)
    full_grad = lax.all_gather(output_gradient, "tensor", axis=1, tiled=True)
    in_grad = (
        widened_gradient
        + lax.dot_general(
            full_grad,
            lax.all_gather(frozen_weight, "dp", axis=1, tiled=True),
            (((1,), (1,)), ((), ())),
            preferred_element_type=jnp.float32,
        )
    ).astype(jnp.bfloat16)
    factor_matrix = ADAPTER_SCALE / BLOCK_TOKENS
    grad_down = (
        factor_matrix
        * jnp.einsum(
            "aqw,aqg->awg", backward_block, active_block_rows, preferred_element_type=jnp.float32
        )
    ).astype(jnp.bfloat16)
    grad_up = (
        factor_matrix
        * jnp.einsum("bkr,bko->bro", lowrank_b, grad_blocks, preferred_element_type=jnp.float32)
    ).astype(jnp.bfloat16)
    slot_range = jnp.arange(per_holder_sums, dtype=jnp.int32)
    base_slot = own_index * per_holder_sums
    piece_down = lax.all_gather(grad_down, "dp", axis=0, tiled=True)
    piece_up = lax.all_gather(grad_up, "dp", axis=0, tiled=True)
    slot_local = adapter_slot_index[block_adapter_index] - base_slot
    chooser = (slot_local[:, None] == slot_range[None, :]).astype(jnp.bfloat16)
    new_down = jnp.einsum("ns,nrd->srd", chooser, piece_down, preferred_element_type=jnp.float32)
    new_up = jnp.einsum("ns,nro->sro", chooser, piece_up, preferred_element_type=jnp.float32)
    return (in_grad, new_down, new_up)


def solution(mesh):
    dp, tensor = mesh.shape["dp"], mesh.shape["tensor"]

    def step(acts, og, w, down, up, blocks, slots):
        if dp == tensor == 4:
            return fused(dp, tensor, acts, og, w, down, up, blocks, slots)
        return per_device(acts, og, w, down, up, blocks, slots)

    return jax.shard_map(
        step,
        mesh=mesh,
        in_specs=(
            P(("groups", "dp"), "tensor"),
            P(("groups", "dp"), "tensor"),
            P("tensor", "dp"),
            P("dp", None, "tensor"),
            P("dp", None, "tensor"),
            P("groups"),
            P(),
        ),
        out_specs=(
            P(("groups", "dp"), "tensor"),
            P(("groups", "dp"), None, "tensor"),
            P(("groups", "dp"), None, "tensor"),
        ),
        check_vma=False,
    )
```

```python
import functools

import jax
import jax.numpy as jnp
from jax import lax
from jax.experimental import pallas as pl
from jax.experimental.pallas import tpu as pltpu
from jax.sharding import PartitionSpec as P

BLOCK_TOKENS = 128


ADAPTER_SCALE = 2.0


MESH = pl.DeviceIdType.MESH
NT = (((1,), (1,)), ((), ()))
NN = (((1,), (0,)), ((), ()))
RANK = 16


def chain_order(dp):
    table = []
    for own in range(dp):
        up, down = list(range(dp - 1, own, -1)), list(range(own))
        first, second = (up, down) if len(up) >= len(down) else (down, up)
        merged = []
        while first or second:
            if first:
                merged.append(first.pop(0))
            if second:
                merged.append(second.pop(0))
        table.append(merged)
    return table


def fused_kernel(
    dp, tensor, chunks,
    block_ref, slot_ref, acts_hbm, og_hbm, w_hbm, down_hbm, up_hbm,
    grad_ref, own_down_ref, own_up_ref,
    acts_ref, og_ref, w_ref, down_ref, up_ref,
    og_all, partial, arrived, total, own_total, sel_send, sel_recv, rank_mine, rank_recv, pieces,
    load_sem, og_send, og_near, og_far, og_relay, og_recv,
    sel_ssem, sel_rsem, rank_ssem, rank_rsem, piece_ssem, piece_rsem, part_ssem, part_rsem,
):
    d, t = lax.axis_index("dp"), lax.axis_index("tensor")
    rows, in_cols = acts_ref.shape
    nblk = rows // BLOCK_TOKENS
    nslot = down_ref.shape[0]
    quarter, half = rows // tensor, rows // 2
    width = in_cols // chunks
    sib, across = t + 1 - 2 * (t % 2), (t + 2) % tensor
    across_sib = across + 1 - 2 * (across % 2)
    x = t // 2

    table = chain_order(dp)
    order = []
    for k in range(dp - 1):
        at = jnp.int32(table[0][k])
        for i in range(1, dp):
            at = jnp.where(d == i, table[i][k], at)
        order.append(at)

    def wait(ref, sem):
        pltpu.make_async_copy(ref, ref, sem).wait()

    def send(src, dst, ssem, rsem, to):
        copy = pltpu.make_async_remote_copy(
            src_ref=src, dst_ref=dst, send_sem=ssem, recv_sem=rsem, device_id=to, device_id_type=MESH
        )
        copy.start()
        return copy

    loads = [
        pltpu.make_async_copy(src, dst, load_sem.at[i])
        for i, (src, dst) in enumerate(
            ((down_hbm, down_ref), (up_hbm, up_ref), (w_hbm, w_ref), (acts_hbm, acts_ref), (og_hbm, og_ref))
        )
    ]
    for load in loads:
        load.start()

    barrier = pltpu.get_barrier_semaphore()
    for i in range(1, dp * tensor):
        peer = (d * tensor + t + i) % (dp * tensor)
        pl.semaphore_signal(
            barrier, inc=1, device_id={"dp": peer // tensor, "tensor": peer % tensor}, device_id_type=MESH
        )
    pl.semaphore_wait(barrier, dp * tensor - 1)

    def og_rows(q):
        return pl.ds(pl.multiple_of(q * quarter, quarter), quarter)

    stays = [jnp.logical_and(t == d, t == q) for q in range(tensor)]
    for q in range(tensor):
        src, dst = og_hbm.at[og_rows(q)], og_all.at[d, og_rows(q)]

        @pl.when(stays[q])
        def _():
            pltpu.make_async_copy(src, dst, og_recv.at[d, q]).start()

        @pl.when(jnp.logical_not(stays[q]))
        def _():
            send(src, dst, og_send.at[q], og_recv.at[d, q], {"dp": t, "tensor": q})

    slots = [slot_ref[block_ref[b]] for b in range(dp * nblk)]
    loads[0].wait()
    loads[1].wait()
    for b in range(dp * nblk):
        here = slots[b] - d * nslot
        own = jnp.logical_and(here >= 0, here < nslot)
        at = jnp.clip(here, 0, nslot - 1)
        dn, up = down_ref[at], up_ref[at]
        r = pl.ds((b % nblk) * RANK, RANK)
        sel_send[b // nblk, r, :in_cols] = jnp.where(own, dn, jnp.zeros_like(dn))
        sel_send[b // nblk, r, in_cols:] = jnp.where(own, up, jnp.zeros_like(up))
    waits = []

    fetch_order = order + [d]
    for k, row in enumerate(fetch_order):
        piece = og_all.at[row, og_rows(t)]
        wait(piece, og_recv.at[row, t])
        waits.append(send(piece, piece, og_near.at[k], og_recv.at[row, t], {"tensor": sib}))
        waits.append(send(piece, piece, og_far.at[k], og_recv.at[row, t], {"tensor": across}))

    for j in range(1, dp):
        peer = (d + j) % dp
        waits.append(send(sel_send.at[peer], sel_recv.at[d], sel_ssem.at[j - 1], sel_rsem.at[d], {"dp": peer}))

    def half_rows(h):
        place = x if h == 0 else 1 - x
        return pl.ds(pl.multiple_of(place * half, half), half)

    def relay_sums(k, h):
        row = order[k]
        wait(og_all.at[row, og_rows(sib if h == 0 else across_sib)], og_recv.at[row, sib if h == 0 else across_sib])
        upward = row > d
        fed = jnp.logical_or(jnp.logical_and(upward, d > 0), jnp.logical_and(row < d, d < dp - 1))
        to = jnp.where(upward, d + 1, d - 1)
        lands = jnp.where(row == d - 1, dp, row)

        @pl.loop(0, chunks)
        def _(c):
            i = h * chunks + c
            tile = w_ref[pl.ds(pl.multiple_of(c * width, width), width), :]
            total[...] = lax.dot_general(
                og_all[row, half_rows(h), :], tile, NT, preferred_element_type=jnp.float32
            )

            @pl.when(fed)
            def _():
                wait(arrived.at[row, i], part_rsem.at[row, i])
                total[...] += arrived[row, i].astype(jnp.float32)

            partial[k, i] = total[...].astype(jnp.bfloat16)
            send(partial.at[k, i], arrived.at[lands, i], part_ssem.at[k, i], part_rsem.at[lands, i], {"dp": to})

    loads[2].wait()
    relay_sums(0, 0)

    for k, row in enumerate(fetch_order):
        piece = og_all.at[row, og_rows(across)]
        wait(piece, og_recv.at[row, across])
        waits.append(send(piece, piece, og_relay.at[k], og_recv.at[row, across], {"tensor": sib}))

    relay_sums(1, 0)

    loads[3].wait()
    loads[4].wait()
    sel = sel_send[d]
    for j in range(1, dp):
        peer = (d + j) % dp
        wait(sel_recv.at[peer], sel_rsem.at[peer])
        sel = sel + sel_recv[peer]
    sel_recv[d] = sel
    for c in range(nblk):
        r, tok = pl.ds(c * RANK, RANK), pl.ds(c * BLOCK_TOKENS, BLOCK_TOKENS)
        low = lax.dot_general(sel_recv[d, r, :in_cols], acts_ref[tok, :], NT, preferred_element_type=jnp.float32)
        back = lax.dot_general(sel_recv[d, r, in_cols:], og_ref[tok, :], NT, preferred_element_type=jnp.float32)
        rank_mine[pl.ds(c * RANK, RANK), :] = low
        rank_mine[pl.ds((nblk + c) * RANK, RANK), :] = back
    for j in range(1, tensor):
        peer = (t + j) % tensor
        waits.append(send(rank_mine, rank_recv.at[t], rank_ssem.at[j - 1], rank_rsem.at[t], {"tensor": peer}))

    relay_sums(2, 0)

    rank = rank_mine[...]
    for j in range(1, tensor):
        peer = (t + j) % tensor
        wait(rank_recv.at[peer], rank_rsem.at[peer])
        rank = rank + rank_recv[peer]
    rank_b = rank.astype(jnp.bfloat16)
    factor = ADAPTER_SCALE / BLOCK_TOKENS
    back_t = []
    for c in range(nblk):
        tok = pl.ds(c * BLOCK_TOKENS, BLOCK_TOKENS)
        low_b = rank_b[c * RANK:(c + 1) * RANK, :]
        back_b = rank_b[(nblk + c) * RANK:(nblk + c + 1) * RANK, :]
        pieces[d, pl.ds(c * RANK, RANK), :in_cols] = (
            factor * lax.dot_general(back_b, acts_ref[tok, :], NN, preferred_element_type=jnp.float32)
        ).astype(jnp.bfloat16)
        pieces[d, pl.ds(c * RANK, RANK), in_cols:] = (
            factor * lax.dot_general(low_b, og_ref[tok, :], NN, preferred_element_type=jnp.float32)
        ).astype(jnp.bfloat16)
        back_t.append(rank[(nblk + c) * RANK:(nblk + c + 1) * RANK, :].T.astype(jnp.bfloat16))

    def pass_on(j, take, give):
        for way, (has, more, step) in enumerate(((d >= j, d < dp - 1, 1), (d + j < dp, d > 0, -1))):
            at = jnp.clip(d - step * j, 0, dp - 1)

            if take:
                @pl.when(has)
                def _():
                    wait(pieces.at[at], piece_rsem.at[at])

            if give is not None:
                @pl.when(jnp.logical_and(has, more))
                def _():
                    if give:
                        send(
                            pieces.at[at], pieces.at[at], piece_ssem.at[way, j], piece_rsem.at[at],
                            {"dp": jnp.clip(d + step, 0, dp - 1)},
                        )
                    else:
                        wait(pieces.at[at], piece_ssem.at[way, j])

    pass_on(0, False, True)
    for k in range(dp - 1):
        relay_sums(k, 1)
        pass_on(k + 1, True, True if k + 1 < dp - 1 else None)

    for q in (sib, across_sib):
        wait(og_all.at[d, og_rows(q)], og_recv.at[d, q])
    for c in range(chunks):
        cols = pl.ds(c * width, width)
        own_total[:, cols] = lax.dot_general(
            og_all[d], w_ref[cols, :], NT, preferred_element_type=jnp.float32
        )
        for i in range(nblk):
            tok = pl.ds(i * BLOCK_TOKENS, BLOCK_TOKENS)
            own_total[tok, cols] += ADAPTER_SCALE * lax.dot_general(
                back_t[i], sel_recv[d, pl.ds(i * RANK, RANK), cols], NN, preferred_element_type=jnp.float32
            )

    shape = (nslot * RANK, nblk * RANK)
    line, column = lax.broadcasted_iota(jnp.int32, shape, 0), lax.broadcasted_iota(jnp.int32, shape, 1)
    choosers = []
    for r in range(dp):
        goal = jnp.full(shape, -1, jnp.int32)
        for b in range(nblk):
            goal = jnp.where(
                column // RANK == b, (slots[r * nblk + b] - d * nslot) * RANK + column % RANK, goal
            )
        choosers.append(jnp.where(goal == line, 1.0, 0.0).astype(jnp.bfloat16))
    chooser = jnp.concatenate(choosers, axis=1)
    all_pieces = pieces[...].reshape(dp * nblk * RANK, pieces.shape[2])
    own_down_ref[...] = lax.dot_general(chooser, all_pieces[:, :in_cols], NN, preferred_element_type=jnp.float32)
    own_up_ref[...] = lax.dot_general(chooser, all_pieces[:, in_cols:], NN, preferred_element_type=jnp.float32)

    for h in range(2):
        for c in range(chunks):
            i, cols = h * chunks + c, pl.ds(c * width, width)
            spot = half_rows(h)

            @pl.when(d > 0)
            def _():
                wait(arrived.at[d, i], part_rsem.at[d, i])
                own_total[spot, cols] += arrived[d, i].astype(jnp.float32)

            @pl.when(d < dp - 1)
            def _():
                wait(arrived.at[dp, i], part_rsem.at[dp, i])
                own_total[spot, cols] += arrived[dp, i].astype(jnp.float32)

            grad_ref[spot, cols] = own_total[spot, cols].astype(jnp.bfloat16)

    for copy in waits:
        copy.wait_send()
    for j in range(dp - 1):
        pass_on(j, False, False)
    for q in range(tensor):
        @pl.when(jnp.logical_not(stays[q]))
        def _():
            wait(og_ref.at[og_rows(q)], og_send.at[q])
    for k in range(dp - 1):
        for c in range(2 * chunks):
            wait(partial.at[k, c], part_ssem.at[k, c])


def fused(dp, tensor, acts, og, w, down, up, blocks, slots):
    rows, in_cols = acts.shape
    out_cols = og.shape[1]
    nslot, nblk, chunks = down.shape[0], rows // BLOCK_TOKENS, 4
    width, half = in_cols // chunks, rows // 2
    vmem, smem = pl.BlockSpec(memory_space=pltpu.VMEM), pl.BlockSpec(memory_space=pltpu.SMEM)
    hbm = pl.BlockSpec(memory_space=pltpu.HBM)
    dma = pltpu.SemaphoreType.DMA
    grad, own_down, own_up = pl.pallas_call(
        functools.partial(fused_kernel, dp, tensor, chunks),
        out_shape=(
            jax.ShapeDtypeStruct((rows, in_cols), jnp.bfloat16),
            jax.ShapeDtypeStruct((nslot * RANK, in_cols), jnp.float32),
            jax.ShapeDtypeStruct((nslot * RANK, out_cols), jnp.float32),
        ),
        in_specs=[smem, smem] + [hbm] * 5,
        out_specs=(vmem, vmem, vmem),
        scratch_shapes=[
            pltpu.VMEM(acts.shape, jnp.bfloat16),
            pltpu.VMEM(og.shape, jnp.bfloat16),
            pltpu.VMEM(w.shape, jnp.bfloat16),
            pltpu.VMEM(down.shape, jnp.bfloat16),
            pltpu.VMEM(up.shape, jnp.bfloat16),
            pltpu.VMEM((dp, rows, w.shape[1]), jnp.bfloat16),
            pltpu.VMEM((dp - 1, 2 * chunks, half, width), jnp.bfloat16),
            pltpu.VMEM((dp + 1, 2 * chunks, half, width), jnp.bfloat16),
            pltpu.VMEM((half, width), jnp.float32),
            pltpu.VMEM((rows, in_cols), jnp.float32),
            pltpu.VMEM((dp, nblk * RANK, in_cols + out_cols), jnp.bfloat16),
            pltpu.VMEM((dp, nblk * RANK, in_cols + out_cols), jnp.bfloat16),
            pltpu.VMEM((2 * nblk * RANK, BLOCK_TOKENS), jnp.float32),
            pltpu.VMEM((tensor, 2 * nblk * RANK, BLOCK_TOKENS), jnp.float32),
            pltpu.VMEM((dp, nblk * RANK, in_cols + out_cols), jnp.bfloat16),
            dma((5,)), dma((tensor,)), dma((dp,)), dma((dp,)), dma((dp,)), dma((dp, tensor)),
            dma((dp - 1,)), dma((dp,)), dma((tensor - 1,)), dma((tensor,)),
            dma((2, dp - 1)), dma((dp,)), dma((dp - 1, 2 * chunks)), dma((dp + 1, 2 * chunks)),
        ],
        compiler_params=pltpu.CompilerParams(
            collective_id=0, has_side_effects=True, vmem_limit_bytes=58 * 1024 * 1024
        ),
        cost_estimate=pl.CostEstimate(
            flops=2 * dp * rows * in_cols * w.shape[1], bytes_accessed=12 * 1024 * 1024, transcendentals=0
        ),
    )(blocks, slots, acts, og, w, down, up)
    return grad, own_down.reshape(nslot, RANK, in_cols), own_up.reshape(nslot, RANK, out_cols)


def per_device(
    acts,
    output_gradient,
    frozen_weight,
    adapter_down_weights,
    adapter_up_weights,
    block_adapter_index,
    adapter_slot_index,
):
    tok_rows, in_cols = acts.shape
    out_cols = output_gradient.shape[1]
    blocks_dev = tok_rows // BLOCK_TOKENS
    own_index = lax.axis_index("dp")
    per_holder_sums = adapter_down_weights.shape[0]
    my_blocks = lax.dynamic_slice_in_dim(block_adapter_index, own_index * blocks_dev, blocks_dev)
    all_down, all_up = (
        lax.all_gather(adapter_down_weights, "dp", axis=0, tiled=True),
        lax.all_gather(adapter_up_weights, "dp", axis=0, tiled=True),
    )
    my_slots = adapter_slot_index[my_blocks]
    selected_down = all_down[my_slots]
    up_sel = all_up[my_slots]
    active_block_rows = acts.reshape(blocks_dev, BLOCK_TOKENS, in_cols)
    grad_blocks = output_gradient.reshape(blocks_dev, BLOCK_TOKENS, out_cols)
    down_portion = jnp.einsum(
        "ctx,cyx->cty", active_block_rows, selected_down, preferred_element_type=jnp.float32
    )
    up_part = jnp.einsum("bko,bro->bkr", grad_blocks, up_sel, preferred_element_type=jnp.float32)
    reduced_rank_output, back_rank = lax.psum((down_portion, up_part), "tensor")
    lowrank_b = reduced_rank_output.astype(jnp.bfloat16)
    backward_block = back_rank.astype(jnp.bfloat16)
    widened_gradient = ADAPTER_SCALE * jnp.einsum(
        "aex,axq->aeq", backward_block, selected_down, preferred_element_type=jnp.float32
    )
    widened_gradient = widened_gradient.reshape(tok_rows, in_cols)
    full_grad = lax.all_gather(output_gradient, "tensor", axis=1, tiled=True)
    in_grad = (
        widened_gradient
        + lax.dot_general(
            full_grad,
            lax.all_gather(frozen_weight, "dp", axis=1, tiled=True),
            (((1,), (1,)), ((), ())),
            preferred_element_type=jnp.float32,
        )
    ).astype(jnp.bfloat16)
    factor_matrix = ADAPTER_SCALE / BLOCK_TOKENS
    grad_down = (
        factor_matrix
        * jnp.einsum(
            "aqw,aqg->awg", backward_block, active_block_rows, preferred_element_type=jnp.float32
        )
    ).astype(jnp.bfloat16)
    grad_up = (
        factor_matrix
        * jnp.einsum("bkr,bko->bro", lowrank_b, grad_blocks, preferred_element_type=jnp.float32)
    ).astype(jnp.bfloat16)
    slot_range = jnp.arange(per_holder_sums, dtype=jnp.int32)
    base_slot = own_index * per_holder_sums
    piece_down = lax.all_gather(grad_down, "dp", axis=0, tiled=True)
    piece_up = lax.all_gather(grad_up, "dp", axis=0, tiled=True)
    slot_local = adapter_slot_index[block_adapter_index] - base_slot
    chooser = (slot_local[:, None] == slot_range[None, :]).astype(jnp.bfloat16)
    new_down = jnp.einsum("ns,nrd->srd", chooser, piece_down, preferred_element_type=jnp.float32)
    new_up = jnp.einsum("ns,nro->sro", chooser, piece_up, preferred_element_type=jnp.float32)
    return (in_grad, new_down, new_up)


def solution(mesh):
    dp, tensor = mesh.shape["dp"], mesh.shape["tensor"]

    def step(acts, og, w, down, up, blocks, slots):
        if dp == tensor == 4:
            return fused(dp, tensor, acts, og, w, down, up, blocks, slots)
        return per_device(acts, og, w, down, up, blocks, slots)

    return jax.shard_map(
        step,
        mesh=mesh,
        in_specs=(
            P(("groups", "dp"), "tensor"),
            P(("groups", "dp"), "tensor"),
            P("tensor", "dp"),
            P("dp", None, "tensor"),
            P("dp", None, "tensor"),
            P("groups"),
            P(),
        ),
        out_specs=(
            P(("groups", "dp"), "tensor"),
            P(("groups", "dp"), None, "tensor"),
            P(("groups", "dp"), None, "tensor"),
        ),
        check_vma=False,
    )
```

```python
import functools

import jax
import jax.numpy as jnp
from jax import lax
from jax.experimental import pallas as pl
from jax.experimental.pallas import tpu as pltpu
from jax.sharding import PartitionSpec as P

BLOCK_TOKENS = 128


ADAPTER_SCALE = 2.0


MESH = pl.DeviceIdType.MESH
NT = (((1,), (1,)), ((), ()))
NN = (((1,), (0,)), ((), ()))
RANK = 16


def chain_order(dp):
    table = []
    for own in range(dp):
        up, down = list(range(dp - 1, own, -1)), list(range(own))
        first, second = (up, down) if len(up) >= len(down) else (down, up)
        merged = []
        while first or second:
            if first:
                merged.append(first.pop(0))
            if second:
                merged.append(second.pop(0))
        table.append(merged)
    return table


def fused_kernel(
    dp, tensor, chunks,
    block_ref, slot_ref, acts_hbm, og_hbm, w_hbm, down_hbm, up_hbm,
    grad_ref, own_down_ref, own_up_ref,
    acts_ref, og_ref, w_ref, down_ref, up_ref,
    og_all, partial, arrived, total, own_total, sel_send, sel_recv, rank_mine, rank_recv, pieces,
    load_sem, og_send, og_near, og_far, og_relay, og_recv,
    sel_ssem, sel_rsem, rank_ssem, rank_rsem, piece_ssem, piece_rsem, part_ssem, part_rsem,
):
    d, t = lax.axis_index("dp"), lax.axis_index("tensor")
    rows, in_cols = acts_ref.shape
    nblk = rows // BLOCK_TOKENS
    nslot = down_ref.shape[0]
    quarter, half = rows // tensor, rows // 2
    width = in_cols // chunks
    sib, across = t + 1 - 2 * (t % 2), (t + 2) % tensor
    across_sib = across + 1 - 2 * (across % 2)
    x = t // 2

    table = chain_order(dp)
    order = []
    for k in range(dp - 1):
        at = jnp.int32(table[0][k])
        for i in range(1, dp):
            at = jnp.where(d == i, table[i][k], at)
        order.append(at)

    def wait(ref, sem):
        pltpu.make_async_copy(ref, ref, sem).wait()

    def send(src, dst, ssem, rsem, to):
        copy = pltpu.make_async_remote_copy(
            src_ref=src, dst_ref=dst, send_sem=ssem, recv_sem=rsem, device_id=to, device_id_type=MESH
        )
        copy.start()
        return copy

    loads = [
        pltpu.make_async_copy(src, dst, load_sem.at[i])
        for i, (src, dst) in enumerate(
            ((down_hbm, down_ref), (up_hbm, up_ref), (w_hbm, w_ref), (acts_hbm, acts_ref), (og_hbm, og_ref))
        )
    ]
    for load in loads:
        load.start()

    barrier = pltpu.get_barrier_semaphore()
    for i in range(1, dp * tensor):
        peer = (d * tensor + t + i) % (dp * tensor)
        pl.semaphore_signal(
            barrier, inc=1, device_id={"dp": peer // tensor, "tensor": peer % tensor}, device_id_type=MESH
        )
    pl.semaphore_wait(barrier, dp * tensor - 1)

    def og_rows(q):
        return pl.ds(pl.multiple_of(q * quarter, quarter), quarter)

    stays = [jnp.logical_and(t == d, t == q) for q in range(tensor)]
    for q in range(tensor):
        src, dst = og_hbm.at[og_rows(q)], og_all.at[d, og_rows(q)]

        @pl.when(stays[q])
        def _():
            pltpu.make_async_copy(src, dst, og_recv.at[d, q]).start()

        @pl.when(jnp.logical_not(stays[q]))
        def _():
            send(src, dst, og_send.at[q], og_recv.at[d, q], {"dp": t, "tensor": q})

    slots = [slot_ref[block_ref[b]] for b in range(dp * nblk)]
    loads[0].wait()
    loads[1].wait()
    for b in range(dp * nblk):
        here = slots[b] - d * nslot
        own = jnp.logical_and(here >= 0, here < nslot)
        at = jnp.clip(here, 0, nslot - 1)
        dn, up = down_ref[at], up_ref[at]
        r = pl.ds((b % nblk) * RANK, RANK)
        sel_send[b // nblk, r, :in_cols] = jnp.where(own, dn, jnp.zeros_like(dn))
        sel_send[b // nblk, r, in_cols:] = jnp.where(own, up, jnp.zeros_like(up))
    waits = []

    fetch_order = order + [d]
    for k, row in enumerate(fetch_order):
        piece = og_all.at[row, og_rows(t)]
        wait(piece, og_recv.at[row, t])
        waits.append(send(piece, piece, og_near.at[k], og_recv.at[row, t], {"tensor": sib}))
        waits.append(send(piece, piece, og_far.at[k], og_recv.at[row, t], {"tensor": across}))

    for j in range(1, dp):
        peer = (d + j) % dp
        waits.append(send(sel_send.at[peer], sel_recv.at[d], sel_ssem.at[j - 1], sel_rsem.at[d], {"dp": peer}))

    def half_rows(h):
        place = x if h == 0 else 1 - x
        return pl.ds(pl.multiple_of(place * half, half), half)

    def relay_sums(k, h):
        row = order[k]
        wait(og_all.at[row, og_rows(sib if h == 0 else across_sib)], og_recv.at[row, sib if h == 0 else across_sib])
        upward = row > d
        fed = jnp.logical_or(jnp.logical_and(upward, d > 0), jnp.logical_and(row < d, d < dp - 1))
        to = jnp.where(upward, d + 1, d - 1)
        lands = jnp.where(row == d - 1, dp, row)

        @pl.loop(0, chunks)
        def _(c):
            i = h * chunks + c
            tile = w_ref[pl.ds(pl.multiple_of(c * width, width), width), :]
            total[...] = lax.dot_general(
                og_all[row, half_rows(h), :], tile, NT, preferred_element_type=jnp.float32
            )

            @pl.when(fed)
            def _():
                wait(arrived.at[row, i], part_rsem.at[row, i])
                total[...] += arrived[row, i].astype(jnp.float32)

            partial[k, i] = total[...].astype(jnp.bfloat16)
            send(partial.at[k, i], arrived.at[lands, i], part_ssem.at[k, i], part_rsem.at[lands, i], {"dp": to})

    loads[2].wait()
    relay_sums(0, 0)

    for k, row in enumerate(fetch_order):
        piece = og_all.at[row, og_rows(across)]
        wait(piece, og_recv.at[row, across])
        waits.append(send(piece, piece, og_relay.at[k], og_recv.at[row, across], {"tensor": sib}))

    relay_sums(1, 0)

    loads[3].wait()
    loads[4].wait()
    sel = sel_send[d]
    for j in range(1, dp):
        peer = (d + j) % dp
        wait(sel_recv.at[peer], sel_rsem.at[peer])
        sel = sel + sel_recv[peer]
    sel_recv[d] = sel
    for c in range(nblk):
        r, tok = pl.ds(c * RANK, RANK), pl.ds(c * BLOCK_TOKENS, BLOCK_TOKENS)
        low = lax.dot_general(sel_recv[d, r, :in_cols], acts_ref[tok, :], NT, preferred_element_type=jnp.float32)
        back = lax.dot_general(sel_recv[d, r, in_cols:], og_ref[tok, :], NT, preferred_element_type=jnp.float32)
        rank_mine[pl.ds(c * RANK, RANK), :] = low
        rank_mine[pl.ds((nblk + c) * RANK, RANK), :] = back
    for j in range(1, tensor):
        peer = (t + j) % tensor
        waits.append(send(rank_mine, rank_recv.at[t], rank_ssem.at[j - 1], rank_rsem.at[t], {"tensor": peer}))

    relay_sums(2, 0)

    rank = rank_mine[...]
    for j in range(1, tensor):
        peer = (t + j) % tensor
        wait(rank_recv.at[peer], rank_rsem.at[peer])
        rank = rank + rank_recv[peer]
    rank_b = rank.astype(jnp.bfloat16)
    factor = ADAPTER_SCALE / BLOCK_TOKENS
    back_t = []
    for c in range(nblk):
        tok = pl.ds(c * BLOCK_TOKENS, BLOCK_TOKENS)
        low_b = rank_b[c * RANK:(c + 1) * RANK, :]
        back_b = rank_b[(nblk + c) * RANK:(nblk + c + 1) * RANK, :]
        pieces[d, pl.ds(c * RANK, RANK), :in_cols] = (
            factor * lax.dot_general(back_b, acts_ref[tok, :], NN, preferred_element_type=jnp.float32)
        ).astype(jnp.bfloat16)
        pieces[d, pl.ds(c * RANK, RANK), in_cols:] = (
            factor * lax.dot_general(low_b, og_ref[tok, :], NN, preferred_element_type=jnp.float32)
        ).astype(jnp.bfloat16)
        back_t.append(rank[(nblk + c) * RANK:(nblk + c + 1) * RANK, :].T.astype(jnp.bfloat16))

    def pass_on(j, take, give):
        for way, (has, more, step) in enumerate(((d >= j, d < dp - 1, 1), (d + j < dp, d > 0, -1))):
            at = jnp.clip(d - step * j, 0, dp - 1)

            if take:
                @pl.when(has)
                def _():
                    wait(pieces.at[at], piece_rsem.at[at])

            if give is not None:
                @pl.when(jnp.logical_and(has, more))
                def _():
                    if give:
                        send(
                            pieces.at[at], pieces.at[at], piece_ssem.at[way, j], piece_rsem.at[at],
                            {"dp": jnp.clip(d + step, 0, dp - 1)},
                        )
                    else:
                        wait(pieces.at[at], piece_ssem.at[way, j])

    pass_on(0, False, True)
    for k in range(dp - 1):
        relay_sums(k, 1)
        pass_on(k + 1, True, True if k + 1 < dp - 1 else None)

    for q in (sib, across_sib):
        wait(og_all.at[d, og_rows(q)], og_recv.at[d, q])
    for c in range(chunks):
        cols = pl.ds(c * width, width)
        own_total[:, cols] = lax.dot_general(
            og_all[d], w_ref[cols, :], NT, preferred_element_type=jnp.float32
        )
        for i in range(nblk):
            tok = pl.ds(i * BLOCK_TOKENS, BLOCK_TOKENS)
            own_total[tok, cols] += ADAPTER_SCALE * lax.dot_general(
                back_t[i], sel_recv[d, pl.ds(i * RANK, RANK), cols], NN, preferred_element_type=jnp.float32
            )

    shape = (nslot * RANK, nblk * RANK)
    line, column = lax.broadcasted_iota(jnp.int32, shape, 0), lax.broadcasted_iota(jnp.int32, shape, 1)
    choosers = []
    for r in range(dp):
        goal = jnp.full(shape, -1, jnp.int32)
        for b in range(nblk):
            goal = jnp.where(
                column // RANK == b, (slots[r * nblk + b] - d * nslot) * RANK + column % RANK, goal
            )
        choosers.append(jnp.where(goal == line, 1.0, 0.0).astype(jnp.bfloat16))
    chooser = jnp.concatenate(choosers, axis=1)
    all_pieces = pieces[...].reshape(dp * nblk * RANK, pieces.shape[2])
    own_down_ref[...] = lax.dot_general(chooser, all_pieces[:, :in_cols], NN, preferred_element_type=jnp.float32)
    own_up_ref[...] = lax.dot_general(chooser, all_pieces[:, in_cols:], NN, preferred_element_type=jnp.float32)

    for h in range(2):
        for c in range(chunks):
            i, cols = h * chunks + c, pl.ds(c * width, width)
            spot = half_rows(h)

            @pl.when(d > 0)
            def _():
                wait(arrived.at[d, i], part_rsem.at[d, i])
                own_total[spot, cols] += arrived[d, i].astype(jnp.float32)

            @pl.when(d < dp - 1)
            def _():
                wait(arrived.at[dp, i], part_rsem.at[dp, i])
                own_total[spot, cols] += arrived[dp, i].astype(jnp.float32)

            grad_ref[spot, cols] = own_total[spot, cols].astype(jnp.bfloat16)

    for copy in waits:
        copy.wait_send()
    for j in range(dp - 1):
        pass_on(j, False, False)
    for q in range(tensor):
        @pl.when(jnp.logical_not(stays[q]))
        def _():
            wait(og_ref.at[og_rows(q)], og_send.at[q])
    for k in range(dp - 1):
        for c in range(2 * chunks):
            wait(partial.at[k, c], part_ssem.at[k, c])


def fused(dp, tensor, acts, og, w, down, up, blocks, slots):
    rows, in_cols = acts.shape
    out_cols = og.shape[1]
    nslot, nblk, chunks = down.shape[0], rows // BLOCK_TOKENS, 8
    width, half = in_cols // chunks, rows // 2
    vmem, smem = pl.BlockSpec(memory_space=pltpu.VMEM), pl.BlockSpec(memory_space=pltpu.SMEM)
    hbm = pl.BlockSpec(memory_space=pltpu.HBM)
    dma = pltpu.SemaphoreType.DMA
    grad, own_down, own_up = pl.pallas_call(
        functools.partial(fused_kernel, dp, tensor, chunks),
        out_shape=(
            jax.ShapeDtypeStruct((rows, in_cols), jnp.bfloat16),
            jax.ShapeDtypeStruct((nslot * RANK, in_cols), jnp.float32),
            jax.ShapeDtypeStruct((nslot * RANK, out_cols), jnp.float32),
        ),
        in_specs=[smem, smem] + [hbm] * 5,
        out_specs=(vmem, vmem, vmem),
        scratch_shapes=[
            pltpu.VMEM(acts.shape, jnp.bfloat16),
            pltpu.VMEM(og.shape, jnp.bfloat16),
            pltpu.VMEM(w.shape, jnp.bfloat16),
            pltpu.VMEM(down.shape, jnp.bfloat16),
            pltpu.VMEM(up.shape, jnp.bfloat16),
            pltpu.VMEM((dp, rows, w.shape[1]), jnp.bfloat16),
            pltpu.VMEM((dp - 1, 2 * chunks, half, width), jnp.bfloat16),
            pltpu.VMEM((dp + 1, 2 * chunks, half, width), jnp.bfloat16),
            pltpu.VMEM((half, width), jnp.float32),
            pltpu.VMEM((rows, in_cols), jnp.float32),
            pltpu.VMEM((dp, nblk * RANK, in_cols + out_cols), jnp.bfloat16),
            pltpu.VMEM((dp, nblk * RANK, in_cols + out_cols), jnp.bfloat16),
            pltpu.VMEM((2 * nblk * RANK, BLOCK_TOKENS), jnp.float32),
            pltpu.VMEM((tensor, 2 * nblk * RANK, BLOCK_TOKENS), jnp.float32),
            pltpu.VMEM((dp, nblk * RANK, in_cols + out_cols), jnp.bfloat16),
            dma((5,)), dma((tensor,)), dma((dp,)), dma((dp,)), dma((dp,)), dma((dp, tensor)),
            dma((dp - 1,)), dma((dp,)), dma((tensor - 1,)), dma((tensor,)),
            dma((2, dp - 1)), dma((dp,)), dma((dp - 1, 2 * chunks)), dma((dp + 1, 2 * chunks)),
        ],
        compiler_params=pltpu.CompilerParams(
            collective_id=0, has_side_effects=True, vmem_limit_bytes=58 * 1024 * 1024
        ),
        cost_estimate=pl.CostEstimate(
            flops=2 * dp * rows * in_cols * w.shape[1], bytes_accessed=12 * 1024 * 1024, transcendentals=0
        ),
    )(blocks, slots, acts, og, w, down, up)
    return grad, own_down.reshape(nslot, RANK, in_cols), own_up.reshape(nslot, RANK, out_cols)


def per_device(
    acts,
    output_gradient,
    frozen_weight,
    adapter_down_weights,
    adapter_up_weights,
    block_adapter_index,
    adapter_slot_index,
):
    tok_rows, in_cols = acts.shape
    out_cols = output_gradient.shape[1]
    blocks_dev = tok_rows // BLOCK_TOKENS
    own_index = lax.axis_index("dp")
    per_holder_sums = adapter_down_weights.shape[0]
    my_blocks = lax.dynamic_slice_in_dim(block_adapter_index, own_index * blocks_dev, blocks_dev)
    all_down, all_up = (
        lax.all_gather(adapter_down_weights, "dp", axis=0, tiled=True),
        lax.all_gather(adapter_up_weights, "dp", axis=0, tiled=True),
    )
    my_slots = adapter_slot_index[my_blocks]
    selected_down = all_down[my_slots]
    up_sel = all_up[my_slots]
    active_block_rows = acts.reshape(blocks_dev, BLOCK_TOKENS, in_cols)
    grad_blocks = output_gradient.reshape(blocks_dev, BLOCK_TOKENS, out_cols)
    down_portion = jnp.einsum(
        "ctx,cyx->cty", active_block_rows, selected_down, preferred_element_type=jnp.float32
    )
    up_part = jnp.einsum("bko,bro->bkr", grad_blocks, up_sel, preferred_element_type=jnp.float32)
    reduced_rank_output, back_rank = lax.psum((down_portion, up_part), "tensor")
    lowrank_b = reduced_rank_output.astype(jnp.bfloat16)
    backward_block = back_rank.astype(jnp.bfloat16)
    widened_gradient = ADAPTER_SCALE * jnp.einsum(
        "aex,axq->aeq", backward_block, selected_down, preferred_element_type=jnp.float32
    )
    widened_gradient = widened_gradient.reshape(tok_rows, in_cols)
    full_grad = lax.all_gather(output_gradient, "tensor", axis=1, tiled=True)
    in_grad = (
        widened_gradient
        + lax.dot_general(
            full_grad,
            lax.all_gather(frozen_weight, "dp", axis=1, tiled=True),
            (((1,), (1,)), ((), ())),
            preferred_element_type=jnp.float32,
        )
    ).astype(jnp.bfloat16)
    factor_matrix = ADAPTER_SCALE / BLOCK_TOKENS
    grad_down = (
        factor_matrix
        * jnp.einsum(
            "aqw,aqg->awg", backward_block, active_block_rows, preferred_element_type=jnp.float32
        )
    ).astype(jnp.bfloat16)
    grad_up = (
        factor_matrix
        * jnp.einsum("bkr,bko->bro", lowrank_b, grad_blocks, preferred_element_type=jnp.float32)
    ).astype(jnp.bfloat16)
    slot_range = jnp.arange(per_holder_sums, dtype=jnp.int32)
    base_slot = own_index * per_holder_sums
    piece_down = lax.all_gather(grad_down, "dp", axis=0, tiled=True)
    piece_up = lax.all_gather(grad_up, "dp", axis=0, tiled=True)
    slot_local = adapter_slot_index[block_adapter_index] - base_slot
    chooser = (slot_local[:, None] == slot_range[None, :]).astype(jnp.bfloat16)
    new_down = jnp.einsum("ns,nrd->srd", chooser, piece_down, preferred_element_type=jnp.float32)
    new_up = jnp.einsum("ns,nro->sro", chooser, piece_up, preferred_element_type=jnp.float32)
    return (in_grad, new_down, new_up)


def solution(mesh):
    dp, tensor = mesh.shape["dp"], mesh.shape["tensor"]

    def step(acts, og, w, down, up, blocks, slots):
        if dp == tensor == 4:
            return fused(dp, tensor, acts, og, w, down, up, blocks, slots)
        return per_device(acts, og, w, down, up, blocks, slots)

    return jax.shard_map(
        step,
        mesh=mesh,
        in_specs=(
            P(("groups", "dp"), "tensor"),
            P(("groups", "dp"), "tensor"),
            P("tensor", "dp"),
            P("dp", None, "tensor"),
            P("dp", None, "tensor"),
            P("groups"),
            P(),
        ),
        out_specs=(
            P(("groups", "dp"), "tensor"),
            P(("groups", "dp"), None, "tensor"),
            P(("groups", "dp"), None, "tensor"),
        ),
        check_vma=False,
    )
```
